256 devices in a mesh: row: 16 (over x, y), col: 16 (over z, core).
Axes of the slice: x: 4, y: 4, z: 8, core: 2. Of those that a mesh axis runs over, the one named last changes fastest.
Arguments:
- tokens: bfloat16 [2048, 14336], P('col', 'row'), may hold values from -6 to 6
- cotangent: bfloat16 [2048, 28672], P('row', 'col'), may hold values from -1.1953125 to 1.1953125
- preact: bfloat16 [2048, 28672], P('row', 'col'), may hold values from -6 to 6
- weight: bfloat16 [14336, 28672], P('row', 'col'), may hold values from -0.046875 to 0.046875
Outputs:
- input_grad: bfloat16 [2048, 14336], P('col', 'row')
- weight_grad: bfloat16 [14336, 28672], P('row', 'col')
The draws below stay inside these ranges and needn't reach their ends.
All inputs are finite; a program needn't handle non-finite values.
Results may differ from the reference program's by a relative error of at most 0.0049.
Values may be sent and summed in bfloat16 or wider, within the bound.
No kernel may reach another device: no remote copies, remote signals or barrier semaphores. Data moves between devices by JAX's collectives and lax.ppermute only.
A program may use at most 128 MiB of HBM per device.

```python
import jax
import jax.numpy as jnp
from jax import lax

D = 14336
FF = 28672
TOKENS = 2048


def level_of(stream_key, shape, split, smallest, high):
    factor_of, own = 1.0, jax.random.fold_in(stream_key, 6)
    for position, blocks in split:
        draws = jnp.exp(jax.random.uniform(jax.random.fold_in(own, position), (blocks,), jnp.float32, smallest / len(split), high / len(split)))
        factor_of = factor_of * jnp.repeat(draws, shape[position] // blocks).reshape([-1 if axis == position else 1 for axis in range(len(shape))])
    return factor_of


def noise(key, extent, spread, limit, shards=(), dtype=jnp.bfloat16):
    loudness = level_of(key, extent, shards, -0.22, 0.18) if shards else 1.0
    result = jax.random.normal(key, extent, jnp.float32) * spread * loudness
    return jnp.minimum(jnp.maximum(result, -limit), limit).astype(dtype)


def setup_inputs(seed: int = 0) -> dict:
    streams_of = jax.random.split(jax.random.key(seed), 5)
    return {
        "tokens": noise(streams_of[0], (TOKENS, D), 1.0, 6.0, ((0, 16), (1, 16))),
        "cotangent": noise(streams_of[1], (TOKENS, FF), 0.2, 1.1953125, ((0, 16), (1, 16))),
        "preact": noise(streams_of[2], (TOKENS, FF), 1.5, 6.0, ((0, 16), (1, 16))),
        "weight": noise(streams_of[3], (D, FF), D ** -0.5, 0.046875, ((0, 16), (1, 16))),
    }


root_two_over_pi = 0.7978845608
cubic_coef = 0.044715


def gelu_slope(preact):
    values = preact.astype(jnp.float32)
    hyper = jnp.tanh(root_two_over_pi * (values + cubic_coef * values * values * values))
    return 0.5 * (1.0 + hyper) + 0.5 * values * (1.0 - hyper * hyper) * root_two_over_pi * (1.0 + 3.0 * cubic_coef * values * values)


def reference(tokens, cotangent, preact, weight):
    grad_pre = (cotangent.astype(jnp.float32) * gelu_slope(preact)).astype(jnp.bfloat16)
    weight_grad = lax.dot_general(tokens, grad_pre, (((0,), (0,)), ((), ())), preferred_element_type=jnp.float32).astype(jnp.bfloat16)
    input_grad = lax.dot_general(grad_pre, weight, (((1,), (1,)), ((), ())), preferred_element_type=jnp.float32).astype(jnp.bfloat16)
    return input_grad, weight_grad
```

```python
import jax
import jax.numpy as jnp
import numpy as np
from jax import lax
from jax.experimental import pallas as pl
from jax.experimental.pallas import tpu as pltpu
from jax.sharding import PartitionSpec as P

root_two_over_pi = 0.7978845608
cubic_coef = 0.044715

ROWS, ZS = 16, 8
ORDER = (
    ((4, 12, 1, 3), (1, 3, 4, 12)),
    ((12, 4, 3, 1), (3, 1, 12, 4)),
)
PLACES, WIDE = 4, 256
MIB = 1024 * 1024
COST = pl.CostEstimate(flops=1_000_000, bytes_accessed=1_000_000, transcendentals=0)


def held():
    table = np.zeros((2, 2, ROWS), np.int32)
    for core in range(2):
        for half in range(2):
            for place in range(ROWS):
                for step in range(4):
                    if place >> step & 1:
                        table[core, half, place] ^= ORDER[core][half][step]
    return table


def places_of(table):
    return np.argsort(table, axis=-1).astype(np.int32)


def permute(value, target, name):
    pairs = []
    for row in range(ROWS):
        for col in range(2 * ZS):
            r, z, c = target(row, col // 2, col % 2)
            pairs.append((row * 2 * ZS + col, r * 2 * ZS + (z % ZS) * 2 + c))
    with jax.named_scope(name):
        return lax.ppermute(value, ("row", "col"), pairs)


def gelu_slope(preact):
    values = preact.astype(jnp.float32)
    hyper = jnp.tanh(root_two_over_pi * (values + cubic_coef * values * values * values))
    return 0.5 * (1.0 + hyper) + 0.5 * values * (1.0 - hyper * hyper) * root_two_over_pi * (
        1.0 + 3.0 * cubic_coef * values * values
    )


def across(value, half, step):
    return permute(value, lambda r, z, c: (r ^ ORDER[c][half][step], z, c), f"x{step}{half}")


def onward(value, name):
    return permute(value, lambda r, z, c: (r, z + 1 - 2 * c, c), name)


def swap(value, name):
    return permute(value, lambda r, z, c: (r, z, 1 - c), name)


def small_kernel(kernel, core, outs, *inputs):
    vmem = pl.BlockSpec(memory_space=pltpu.VMEM)
    return pl.pallas_call(
        lambda core_ref, *refs: kernel(core_ref[0], *refs),
        out_shape=[jax.ShapeDtypeStruct(shape, jnp.bfloat16) for shape in outs],
        in_specs=[pl.BlockSpec(memory_space=pltpu.SMEM)] + [vmem] * len(inputs),
        out_specs=[vmem] * len(outs),
        compiler_params=pltpu.CompilerParams(vmem_limit_bytes=6 * MIB),
        cost_estimate=COST,
        name=kernel.__name__.strip("_"),
    )(core, *inputs)


def pair_up(core, own_ref, other_ref, out_ref):
    out_ref[core] = own_ref[...]
    out_ref[1 - core] = other_ref[...]


def line_up(core, first_ref, second_ref, third_ref, out_ref):
    for i, ref in enumerate((first_ref, second_ref, third_ref)):
        out_ref[2 * i : 2 * i + 2] = ref[...]


def put_together(core, *refs):
    for half in range(2):
        first, second, out = refs[half], refs[2 + half], refs[4 + half]
        size = first.shape[0]
        out[:size] = first[...]
        out[size:] = second[...]


def join(core, own, got):
    rows, units = own[0].shape
    return small_kernel(put_together, core, [(2 * rows, units)] * 2, *own, *got)


def wide(value):
    return value.astype(jnp.float32)


def first_sum(core, mine_ref, got_ref, near_ref, far_ref, out_ref):
    for i in range(2):
        out_ref[i] = (wide(mine_ref[i]) + wide(got_ref[i])).astype(jnp.bfloat16)
    total = wide(mine_ref[core]) + wide(got_ref[core]) + wide(near_ref[0]) + wide(far_ref[0])
    out_ref[core] = total.astype(jnp.bfloat16)


def second_sum(core, mine_ref, got_ref, arrived_ref, out_ref):
    for i in range(2):
        total = wide(mine_ref[2 + i]) + wide(got_ref[2 + i]) + wide(arrived_ref[i])
        out_ref[i] = total.astype(jnp.bfloat16)


def third_sum(core, mine_ref, got_ref, arrived_ref, keep_ref, give_ref):
    for which, out_ref in ((core, keep_ref), (1 - core, give_ref)):
        total = wide(mine_ref[4 + which]) + wide(got_ref[4 + which]) + wide(arrived_ref[which])
        out_ref[...] = total.astype(jnp.bfloat16)


def last_sum(core, mine_ref, got_ref, near_ref, far_ref, out_ref):
    total = wide(mine_ref[6]) + wide(got_ref[6]) + wide(near_ref[...]) + wide(far_ref[...])
    out_ref[...] = total.astype(jnp.bfloat16)


def partial_kernel(firsts, sub, slot_ref, w_ref, *refs):
    count = 2 * len(firsts)
    *out_refs, result, out_sem = refs[-6:]
    for i in range(count):
        half = i % 2
        result[i] = lax.dot_general(
            refs[i][...], w_ref[...], (((1,), (1,)), ((), ())), preferred_element_type=jnp.float32
        ).astype(jnp.bfloat16)
        for p in range(PLACES):
            slot = slot_ref[half * ROWS + firsts[i // 2] + p]
            source = result.at[i, pl.ds(p * sub, sub), :]
            for out_ref, low, high in zip(out_refs, (0, 1, ZS, ZS + 1), (1, ZS, ZS + 1, 2 * ZS)):

                @pl.when((slot >= low) & (slot < high))
                def _():
                    pltpu.make_async_copy(
                        source, out_ref.at[slot - low, pl.ds(half * sub, sub), :], out_sem
                    ).start()

    pltpu.make_async_copy(result, result, out_sem).wait()


def partial_sums(slots, firsts, pieces, weight, into=()):
    sub = pieces[0].shape[0] // PLACES
    features = weight.shape[0]
    count = len(pieces)
    anywhere, vmem = pl.BlockSpec(memory_space=pl.ANY), pl.BlockSpec(memory_space=pltpu.VMEM)
    inputs = (weight, *pieces, *into)
    return pl.pallas_call(
        lambda *refs: partial_kernel(firsts, sub, *refs),
        out_shape=[
            jax.ShapeDtypeStruct((n, 2 * sub, features), jnp.bfloat16)
            for n in (1, ZS - 1, 1, ZS - 1)
        ],
        in_specs=[pl.BlockSpec(memory_space=pltpu.SMEM)]
        + [vmem] * (1 + count)
        + [anywhere] * len(into),
        out_specs=[anywhere] * 4,
        scratch_shapes=[
            pltpu.VMEM((count, PLACES * sub, features), jnp.bfloat16),
            pltpu.SemaphoreType.DMA,
        ],
        input_output_aliases={2 + count + i: i for i in range(len(into))},
        compiler_params=pltpu.CompilerParams(vmem_limit_bytes=10 * MIB),
        cost_estimate=COST,
        name="partial_sums",
    )(slots, *inputs)


def turn_kernel(place_ref, *refs):
    sources, (out_ref, ordered, sem) = refs[:-3], refs[-3:]
    total = ordered.shape[0]
    sub = total // (2 * ROWS)
    index = 0
    for source in sources:
        for b in range(source.shape[0]):
            for half in range(2):
                row = pl.multiple_of(place_ref[index] * sub, sub)
                pltpu.make_async_copy(
                    source.at[b, pl.ds(half * sub, sub), :], ordered.at[pl.ds(row, sub), :], sem
                ).start()
                index += 1
    pltpu.make_async_copy(ordered, ordered, sem).wait()

    def turn(t, carry):
        rows = pl.ds(pl.multiple_of(t * 256, 256), 256)
        out_ref[:, rows] = ordered[rows, :].T
        return carry

    lax.fori_loop(0, total // 256, turn, 0)


def turned_tokens(places, sources):
    features = sources[0].shape[-1]
    total = sum(source.shape[0] * source.shape[1] for source in sources)
    return pl.pallas_call(
        turn_kernel,
        out_shape=jax.ShapeDtypeStruct((features, total), jnp.bfloat16),
        grid_spec=pltpu.PrefetchScalarGridSpec(
            num_scalar_prefetch=1,
            grid=(),
            in_specs=[pl.BlockSpec(memory_space=pl.ANY)] * len(sources),
            out_specs=pl.BlockSpec(memory_space=pltpu.VMEM),
            scratch_shapes=[
                pltpu.VMEM((total, features), jnp.bfloat16),
                pltpu.SemaphoreType.DMA,
            ],
        ),
        compiler_params=pltpu.CompilerParams(vmem_limit_bytes=10 * MIB),
        cost_estimate=pl.CostEstimate(flops=0, bytes_accessed=16_000_000, transcendentals=0),
        name="turned_tokens",
    )(places, *sources)


def weight_kernel(count, turned_ref, *refs):
    pieces, out_ref = refs[:count], refs[-1]
    sums, at = None, 0
    for piece in pieces:
        rows = piece.shape[0]
        term = jnp.dot(
            turned_ref[:, at : at + rows], piece[...], preferred_element_type=jnp.float32
        )
        sums = term if sums is None else sums + term
        at += rows
    out_ref[...] = sums.astype(jnp.bfloat16)


def weight_gradient(turned, pieces, begin, end, into=None):
    features, total = turned.shape
    units = pieces[0].shape[1]
    inputs = (turned, *pieces) + (() if into is None else (into,))
    return pl.pallas_call(
        lambda *refs: weight_kernel(len(pieces), *refs),
        out_shape=jax.ShapeDtypeStruct((features, units), jnp.bfloat16),
        grid=(end - begin,),
        in_specs=[pl.BlockSpec(memory_space=pltpu.VMEM)]
        + [pl.BlockSpec((piece.shape[0], WIDE), lambda n: (0, n + begin)) for piece in pieces]
        + [pl.BlockSpec(memory_space=pl.ANY)] * (into is not None),
        out_specs=pl.BlockSpec((features, WIDE), lambda n: (0, n + begin)),
        input_output_aliases={} if into is None else {1 + len(pieces): 0},
        compiler_params=pltpu.CompilerParams(vmem_limit_bytes=16 * MIB),
        cost_estimate=pl.CostEstimate(
            flops=2 * total * WIDE * (end - begin) * features,
            bytes_accessed=2_000_000 * (end - begin),
            transcendentals=0,
        ),
        name="weight_gradient",
    )(*inputs)


def shards(tokens, cotangent, preact, weight):
    row, col = lax.axis_index("row"), lax.axis_index("col")
    z, core = col // 2, col % 2
    size, features = tokens.shape
    sub = size // 2
    table = held()
    block = row ^ jnp.asarray(table)[core]
    to, parity = (block // 2 - z) % ZS, block % 2
    worker = jnp.where(to % 4 == 0, parity, to // 4)
    away = jnp.where(to > 4, ZS - to, to)
    slot = jnp.where(away == 4, 0, jnp.where(away == 0, 7, 7 - 2 * away + parity))
    slots = jnp.where(worker == core, slot, slot + ZS).reshape(-1).astype(jnp.int32)
    down = 2 * core - 1
    chips = [z] + [z + down * i for i in (1, 2, 3, 4)] + [z - down * i for i in (1, 2, 3)]
    blocks = jnp.stack([(p % ZS) * 2 + c for p in chips for c in range(2)])
    place = jnp.asarray(places_of(table))[core][:, blocks ^ row]
    start = (place // PLACES * 2 + jnp.arange(2)[:, None]) * PLACES + place % PLACES
    starts = start.T.reshape(-1).astype(jnp.int32)

    partner = swap(tokens, "token_pair")
    grad = (cotangent.astype(jnp.float32) * gelu_slope(preact)).astype(jnp.bfloat16)
    own = [grad[:sub], grad[sub:]]
    core = core.reshape(1).astype(jnp.int32)
    own, slots, starts, core = lax.optimization_barrier((own, slots, starts, core))
    got = [across(own[half], half, 0) for half in range(2)]
    (chip,) = small_kernel(pair_up, core, [(2, size, features)], tokens, partner)
    ring = [onward(chip, "tokens1")]
    got = lax.optimization_barrier(got)
    own = join(core, own, got)
    got = [across(own[half], half, 1) for half in range(2)]
    *got, ring[0] = lax.optimization_barrier((*got, ring[0]))
    own = join(core, own, got)
    got = [across(own[half], half, 2) for half in range(2)]
    ring.append(onward(ring[0], "tokens2"))
    sums = partial_sums(slots, (0,), own, weight)
    own, sums = lax.optimization_barrier((own, sums))
    near = [across(own[half], half, 3) for half in range(2)]
    *got, ring[1] = lax.optimization_barrier((*got, ring[1]))
    far = [across(got[half], half, 3) for half in range(2)]
    ring.append(onward(ring[1], "tokens3"))
    sums = partial_sums(slots, (4,), got, weight, into=sums)
    near, ring, sums = lax.optimization_barrier((near, ring, sums))
    ring.append(onward(ring[2], "tokens4"))
    (passed,) = small_kernel(line_up, core, [(6, size, features)], *ring[:3])
    others = swap(passed, "token_swap")
    sums = partial_sums(slots, (8,), near, weight, into=sums)
    far, ring, sums = lax.optimization_barrier((far, ring, sums))
    mine_far, mine, other_far, other = partial_sums(slots, (12,), far, weight, into=sums)
    pieces = [*own, *got, *near, *far]

    near = onward(mine_far, "sums1")
    far = permute(other_far, lambda r, z, c: (r, z - 1 + 2 * c, 1 - c), "sums1x")
    got = swap(other, "sum_swap")
    token_arrays, _ = lax.optimization_barrier(([chip, *ring, others], mine))
    turned = turned_tokens(starts, token_arrays)
    near, far, got, turned = lax.optimization_barrier((near, far, got, turned))
    pair = (2, size, features)
    (running,) = small_kernel(first_sum, core, [pair], mine, got, near, far)
    arrived = onward(running, "sums2")
    turned, _ = lax.optimization_barrier((turned, running))
    weight_grad = weight_gradient(turned, pieces, 0, pieces[0].shape[1] // WIDE)
    arrived, weight_grad = lax.optimization_barrier((arrived, weight_grad))
    (running,) = small_kernel(second_sum, core, [pair], mine, got, arrived)
    arrived = onward(running, "sums3")
    keep, give = small_kernel(third_sum, core, [(size, features)] * 2, mine, got, arrived)
    near = onward(keep, "sums4")
    far = permute(give, lambda r, z, c: (r, z + 1 - 2 * c, 1 - c), "sums4x")
    (input_grad,) = small_kernel(last_sum, core, [(size, features)], mine, got, near, far)
    return input_grad, weight_grad


def solution(mesh):
    placed = (P("col", "row"), P("row", "col"), P("row", "col"), P("row", "col"))
    return jax.shard_map(
        shards,
        mesh=mesh,
        in_specs=placed,
        out_specs=(P("col", "row"), P("row", "col")),
        check_vma=False,
    )
```

```python
import jax
import jax.numpy as jnp
import numpy as np
from jax import lax
from jax.experimental import pallas as pl
from jax.experimental.pallas import tpu as pltpu
from jax.sharding import PartitionSpec as P

root_two_over_pi = 0.7978845608
cubic_coef = 0.044715

ROWS, ZS = 16, 8
ORDER = (
    ((4, 12, 1, 3), (1, 3, 4, 12)),
    ((12, 4, 3, 1), (3, 1, 12, 4)),
)
PLACES, WIDE = 4, 256
MIB = 1024 * 1024
COST = pl.CostEstimate(flops=1_000_000, bytes_accessed=1_000_000, transcendentals=0)


def held():
    table = np.zeros((2, 2, ROWS), np.int32)
    for core in range(2):
        for half in range(2):
            for place in range(ROWS):
                for step in range(4):
                    if place >> step & 1:
                        table[core, half, place] ^= ORDER[core][half][step]
    return table


def places_of(table):
    return np.argsort(table, axis=-1).astype(np.int32)


def permute(value, target, name):
    pairs = []
    for row in range(ROWS):
        for col in range(2 * ZS):
            r, z, c = target(row, col // 2, col % 2)
            pairs.append((row * 2 * ZS + col, r * 2 * ZS + (z % ZS) * 2 + c))
    with jax.named_scope(name):
        return lax.ppermute(value, ("row", "col"), pairs)


def gelu_slope(preact):
    values = preact.astype(jnp.float32)
    hyper = jnp.tanh(root_two_over_pi * (values + cubic_coef * values * values * values))
    return 0.5 * (1.0 + hyper) + 0.5 * values * (1.0 - hyper * hyper) * root_two_over_pi * (
        1.0 + 3.0 * cubic_coef * values * values
    )


def across(value, half, step):
    return permute(value, lambda r, z, c: (r ^ ORDER[c][half][step], z, c), f"x{step}{half}")


def onward(value, name):
    return permute(value, lambda r, z, c: (r, z + 1 - 2 * c, c), name)


def swap(value, name):
    return permute(value, lambda r, z, c: (r, z, 1 - c), name)


def small_kernel(kernel, core, outs, *inputs):
    vmem = pl.BlockSpec(memory_space=pltpu.VMEM)
    return pl.pallas_call(
        lambda core_ref, *refs: kernel(core_ref[0], *refs),
        out_shape=[jax.ShapeDtypeStruct(shape, jnp.bfloat16) for shape in outs],
        in_specs=[pl.BlockSpec(memory_space=pltpu.SMEM)] + [vmem] * len(inputs),
        out_specs=[vmem] * len(outs),
        compiler_params=pltpu.CompilerParams(vmem_limit_bytes=6 * MIB),
        cost_estimate=COST,
        name=kernel.__name__.strip("_"),
    )(core, *inputs)


def pair_up(core, own_ref, other_ref, out_ref):
    out_ref[core] = own_ref[...]
    out_ref[1 - core] = other_ref[...]


def pick_one(core, pair_ref, out_ref):
    out_ref[0] = pair_ref[core]


def line_up(core, *refs):
    *pair_refs, last_ref, out_ref = refs
    for i, ref in enumerate(pair_refs):
        out_ref[2 * i : 2 * i + 2] = ref[...]
    out_ref[2 * len(pair_refs)] = last_ref[0]


def put_together(core, *refs):
    for half in range(2):
        first, second, out = refs[half], refs[2 + half], refs[4 + half]
        size = first.shape[0]
        out[:size] = first[...]
        out[size:] = second[...]


def join(core, own, got):
    rows, units = own[0].shape
    return small_kernel(put_together, core, [(2 * rows, units)] * 2, *own, *got)


def wide(value):
    return value.astype(jnp.float32)


def first_sum(core, mine_ref, got_ref, near_ref, far_ref, out_ref):
    for i in range(2):
        out_ref[i] = (wide(mine_ref[i]) + wide(got_ref[i])).astype(jnp.bfloat16)
    total = wide(mine_ref[core]) + wide(got_ref[core]) + wide(near_ref[0]) + wide(far_ref[0])
    out_ref[core] = total.astype(jnp.bfloat16)


def second_sum(core, mine_ref, got_ref, arrived_ref, out_ref):
    for i in range(2):
        total = wide(mine_ref[2 + i]) + wide(got_ref[2 + i]) + wide(arrived_ref[i])
        out_ref[i] = total.astype(jnp.bfloat16)


def third_sum(core, mine_ref, got_ref, arrived_ref, keep_ref, give_ref):
    for which, out_ref in ((core, keep_ref), (1 - core, give_ref)):
        total = wide(mine_ref[4 + which]) + wide(got_ref[4 + which]) + wide(arrived_ref[which])
        out_ref[...] = total.astype(jnp.bfloat16)


def last_sum(core, mine_ref, got_ref, near_ref, far_ref, out_ref):
    total = wide(mine_ref[6]) + wide(got_ref[6]) + wide(near_ref[...]) + wide(far_ref[...])
    out_ref[...] = total.astype(jnp.bfloat16)


def partial_kernel(parts, sub, slot_ref, w_ref, *refs):
    *out_refs, result, out_sem = refs[-6:]
    for i, (first, half) in enumerate(parts):
        result[i] = lax.dot_general(
            refs[i][...], w_ref[...], (((1,), (1,)), ((), ())), preferred_element_type=jnp.float32
        ).astype(jnp.bfloat16)
        for p in range(PLACES):
            slot = slot_ref[half * ROWS + first + p]
            source = result.at[i, pl.ds(p * sub, sub), :]
            for out_ref, low, high in zip(out_refs, (0, 1, ZS, ZS + 1), (1, ZS, ZS + 1, 2 * ZS)):

                @pl.when((slot >= low) & (slot < high))
                def _():
                    pltpu.make_async_copy(
                        source, out_ref.at[slot - low, pl.ds(half * sub, sub), :], out_sem
                    ).start()

    pltpu.make_async_copy(result, result, out_sem).wait()


def partial_sums(slots, parts, pieces, weight, into=()):
    sub = pieces[0].shape[0] // PLACES
    features = weight.shape[0]
    count = len(pieces)
    anywhere, vmem = pl.BlockSpec(memory_space=pl.ANY), pl.BlockSpec(memory_space=pltpu.VMEM)
    inputs = (weight, *pieces, *into)
    return pl.pallas_call(
        lambda *refs: partial_kernel(parts, sub, *refs),
        out_shape=[
            jax.ShapeDtypeStruct((n, 2 * sub, features), jnp.bfloat16)
            for n in (1, ZS - 1, 1, ZS - 1)
        ],
        in_specs=[pl.BlockSpec(memory_space=pltpu.SMEM)]
        + [vmem] * (1 + count)
        + [anywhere] * len(into),
        out_specs=[anywhere] * 4,
        scratch_shapes=[
            pltpu.VMEM((count, PLACES * sub, features), jnp.bfloat16),
            pltpu.SemaphoreType.DMA,
        ],
        input_output_aliases={2 + count + i: i for i in range(len(into))},
        compiler_params=pltpu.CompilerParams(vmem_limit_bytes=10 * MIB),
        cost_estimate=COST,
        name="partial_sums",
    )(slots, *inputs)


def turn_kernel(place_ref, *refs):
    sources, (out_ref, ordered, sem) = refs[:-3], refs[-3:]
    total = ordered.shape[0]
    sub = total // (2 * ROWS)
    index = 0
    for source in sources:
        for b in range(source.shape[0]):
            for half in range(2):
                row = pl.multiple_of(place_ref[index] * sub, sub)
                pltpu.make_async_copy(
                    source.at[b, pl.ds(half * sub, sub), :], ordered.at[pl.ds(row, sub), :], sem
                ).start()
                index += 1
    pltpu.make_async_copy(ordered, ordered, sem).wait()

    features = ordered.shape[1]
    for at in range(0, features, WIDE):
        size = min(WIDE, features - at)
        place = lambda axis: lax.broadcasted_iota(jnp.int32, (size, size), axis)
        one = jnp.where(place(0) == place(1), 1.0, 0.0).astype(jnp.bfloat16)
        out_ref[at : at + size, :] = lax.dot_general(
            one,
            ordered[:, at : at + size],
            (((1,), (1,)), ((), ())),
            preferred_element_type=jnp.float32,
        ).astype(jnp.bfloat16)


def turned_tokens(places, sources):
    features = sources[0].shape[-1]
    total = sum(source.shape[0] * source.shape[1] for source in sources)
    return pl.pallas_call(
        turn_kernel,
        out_shape=jax.ShapeDtypeStruct((features, total), jnp.bfloat16),
        grid_spec=pltpu.PrefetchScalarGridSpec(
            num_scalar_prefetch=1,
            grid=(),
            in_specs=[pl.BlockSpec(memory_space=pl.ANY)] * len(sources),
            out_specs=pl.BlockSpec(memory_space=pltpu.VMEM),
            scratch_shapes=[
                pltpu.VMEM((total, features), jnp.bfloat16),
                pltpu.SemaphoreType.DMA,
            ],
        ),
        compiler_params=pltpu.CompilerParams(vmem_limit_bytes=10 * MIB),
        cost_estimate=pl.CostEstimate(flops=0, bytes_accessed=16_000_000, transcendentals=0),
        name="turned_tokens",
    )(places, *sources)


def weight_kernel(count, turned_ref, *refs):
    pieces, out_ref = refs[:count], refs[-1]
    sums, at = None, 0
    for piece in pieces:
        rows = piece.shape[0]
        term = jnp.dot(
            turned_ref[:, at : at + rows], piece[...], preferred_element_type=jnp.float32
        )
        sums = term if sums is None else sums + term
        at += rows
    out_ref[...] = sums.astype(jnp.bfloat16)


def weight_gradient(turned, pieces, begin, end, into=None):
    features, total = turned.shape
    units = pieces[0].shape[1]
    inputs = (turned, *pieces) + (() if into is None else (into,))
    return pl.pallas_call(
        lambda *refs: weight_kernel(len(pieces), *refs),
        out_shape=jax.ShapeDtypeStruct((features, units), jnp.bfloat16),
        grid=(end - begin,),
        in_specs=[pl.BlockSpec(memory_space=pltpu.VMEM)]
        + [pl.BlockSpec((piece.shape[0], WIDE), lambda n: (0, n + begin)) for piece in pieces]
        + [pl.BlockSpec(memory_space=pl.ANY)] * (into is not None),
        out_specs=pl.BlockSpec((features, WIDE), lambda n: (0, n + begin)),
        input_output_aliases={} if into is None else {1 + len(pieces): 0},
        compiler_params=pltpu.CompilerParams(vmem_limit_bytes=16 * MIB),
        cost_estimate=pl.CostEstimate(
            flops=2 * total * WIDE * (end - begin) * features,
            bytes_accessed=2_000_000 * (end - begin),
            transcendentals=0,
        ),
        name="weight_gradient",
    )(*inputs)


def shards(tokens, cotangent, preact, weight):
    row, col = lax.axis_index("row"), lax.axis_index("col")
    z, core = col // 2, col % 2
    size, features = tokens.shape
    sub = size // 2
    table = held()
    block = row ^ jnp.asarray(table)[core]
    to, parity = (block // 2 - z) % ZS, block % 2
    worker = jnp.where(to % 4 == 0, parity, to // 4)
    away = jnp.where(to > 4, ZS - to, to)
    slot = jnp.where(away == 4, 0, jnp.where(away == 0, 7, 7 - 2 * away + parity))
    slots = jnp.where(worker == core, slot, slot + ZS).reshape(-1).astype(jnp.int32)
    down = 2 * core - 1
    chips = [z] + [z + down * i for i in (1, 2, 3)]
    blocks = [(p % ZS) * 2 + c for p in chips for c in range(2)] + [(z + 4) % ZS * 2 + core]
    chips = [z - down * i for i in (1, 2, 3)]
    blocks += [(p % ZS) * 2 + c for p in chips for c in range(2)] + [(z + 4) % ZS * 2 + 1 - core]
    place = jnp.asarray(places_of(table))[core][:, jnp.stack(blocks) ^ row]
    start = (place // PLACES * 2 + jnp.arange(2)[:, None]) * PLACES + place % PLACES
    starts = start.T.reshape(-1).astype(jnp.int32)

    partner = swap(tokens, "token_pair")
    core = core.reshape(1).astype(jnp.int32)
    own = []
    for half in range(2):
        rows = slice(half * sub, (half + 1) * sub)
        values, slope_at = cotangent[rows], preact[rows]
        if half:
            values, slope_at, *own = lax.optimization_barrier((values, slope_at, *own))
        own.append((values.astype(jnp.float32) * gelu_slope(slope_at)).astype(jnp.bfloat16))
    got = [across(own[half], half, 0) for half in range(2)]
    (chip,) = small_kernel(pair_up, core, [(2, size, features)], tokens, partner)
    first = [across(own[half], half, 1) for half in range(2)]
    ring = [onward(chip, "tokens1")]
    *got, chip, slots, starts = lax.optimization_barrier((*got, chip, slots, starts))
    second = [across(got[half], half, 1) for half in range(2)]
    own = join(core, own, got)
    early = [across(own[half], half, 2) for half in range(2)]
    first, second, ring[0] = lax.optimization_barrier((first, second, ring[0]))
    got = join(core, first, second)
    own = join(core, own, got)
    late = [across(got[half], half, 2) for half in range(2)]
    ring.append(onward(ring[0], "tokens2"))
    both_halves = lambda first: ((first, 0), (first, 1))
    own, early = lax.optimization_barrier((own, early))
    near = [across(own[half], half, 3) for half in range(2)]
    sums = partial_sums(slots, both_halves(0), own, weight)
    early, late, ring[1], sums = lax.optimization_barrier((early, late, ring[1], sums))
    got = join(core, early, late)
    far = [across(got[half], half, 3) for half in range(2)]
    ring.append(onward(ring[1], "tokens3"))
    sums = partial_sums(slots, both_halves(4), got, weight, into=sums)
    near, sums = lax.optimization_barrier((near, sums))
    sums = partial_sums(slots, both_halves(8), near, weight, into=sums)
    far[0], ring, sums = lax.optimization_barrier((far[0], ring, sums))
    ring.append(
        onward(small_kernel(pick_one, core, [(1, size, features)], ring[2])[0], "tokens4")
    )
    for half in range(2):
        far[half], sums = lax.optimization_barrier((far[half], sums))
        sums = partial_sums(slots, ((12, half),), far[half : half + 1], weight, into=sums)
    mine_far, mine, other_far, other = sums
    pieces = [*own, *got, *near, *far]

    near = onward(mine_far, "sums1")
    far = permute(other_far, lambda r, z, c: (r, z - 1 + 2 * c, 1 - c), "sums1x")
    got = swap(other, "sum_swap")
    (passed,) = small_kernel(line_up, core, [(7, size, features)], *ring)
    others = swap(passed, "token_swap")
    near, far, got, others = lax.optimization_barrier((near, far, got, others))
    pair = (2, size, features)
    (running,) = small_kernel(first_sum, core, [pair], mine, got, near, far)
    arrived = onward(running, "sums2")
    token_arrays, _ = lax.optimization_barrier(([chip, *ring, others], running))
    turned = turned_tokens(starts, token_arrays)
    arrived, turned = lax.optimization_barrier((arrived, turned))
    (running,) = small_kernel(second_sum, core, [pair], mine, got, arrived)
    arrived = onward(running, "sums3")
    turned, _ = lax.optimization_barrier((turned, running))
    weight_grad = weight_gradient(turned, pieces, 0, pieces[0].shape[1] // WIDE)
    arrived, weight_grad = lax.optimization_barrier((arrived, weight_grad))
    keep, give = small_kernel(third_sum, core, [(size, features)] * 2, mine, got, arrived)
    near = onward(keep, "sums4")
    far = permute(give, lambda r, z, c: (r, z + 1 - 2 * c, 1 - c), "sums4x")
    (input_grad,) = small_kernel(last_sum, core, [(size, features)], mine, got, near, far)
    return input_grad, weight_grad


def solution(mesh):
    placed = (P("col", "row"), P("row", "col"), P("row", "col"), P("row", "col"))
    return jax.shard_map(
        shards,
        mesh=mesh,
        in_specs=placed,
        out_specs=(P("col", "row"), P("row", "col")),
        check_vma=False,
    )
```

```python
import jax
import jax.numpy as jnp
import numpy as np
from jax import lax
from jax.experimental import pallas as pl
from jax.experimental.pallas import tpu as pltpu
from jax.sharding import PartitionSpec as P

root_two_over_pi = 0.7978845608
cubic_coef = 0.044715

ROWS, ZS = 16, 8
ORDER = (
    ((4, 12, 1, 3), (1, 3, 4, 12)),
    ((12, 4, 3, 1), (3, 1, 12, 4)),
)
PLACES, WIDE = 4, 256
MIB = 1024 * 1024
COST = pl.CostEstimate(flops=1_000_000, bytes_accessed=1_000_000, transcendentals=0)


def held():
    table = np.zeros((2, 2, ROWS), np.int32)
    for core in range(2):
        for half in range(2):
            for place in range(ROWS):
                for step in range(4):
                    if place >> step & 1:
                        table[core, half, place] ^= ORDER[core][half][step]
    return table


def places_of(table):
    return np.argsort(table, axis=-1).astype(np.int32)


def permute(value, target, name):
    pairs = []
    for row in range(ROWS):
        for col in range(2 * ZS):
            r, z, c = target(row, col // 2, col % 2)
            pairs.append((row * 2 * ZS + col, r * 2 * ZS + (z % ZS) * 2 + c))
    with jax.named_scope(name):
        return lax.ppermute(value, ("row", "col"), pairs)


def gelu_slope(preact):
    values = preact.astype(jnp.float32)
    hyper = jnp.tanh(root_two_over_pi * (values + cubic_coef * values * values * values))
    return 0.5 * (1.0 + hyper) + 0.5 * values * (1.0 - hyper * hyper) * root_two_over_pi * (
        1.0 + 3.0 * cubic_coef * values * values
    )


def across(value, half, step):
    return permute(value, lambda r, z, c: (r ^ ORDER[c][half][step], z, c), f"x{step}{half}")


def onward(value, name):
    return permute(value, lambda r, z, c: (r, z + 1 - 2 * c, c), name)


def swap(value, name):
    return permute(value, lambda r, z, c: (r, z, 1 - c), name)


def small_kernel(kernel, core, outs, *inputs):
    vmem = pl.BlockSpec(memory_space=pltpu.VMEM)
    return pl.pallas_call(
        lambda core_ref, *refs: kernel(core_ref[0], *refs),
        out_shape=[jax.ShapeDtypeStruct(shape, jnp.bfloat16) for shape in outs],
        in_specs=[pl.BlockSpec(memory_space=pltpu.SMEM)] + [vmem] * len(inputs),
        out_specs=[vmem] * len(outs),
        compiler_params=pltpu.CompilerParams(vmem_limit_bytes=6 * MIB),
        cost_estimate=COST,
        name=kernel.__name__.strip("_"),
    )(core, *inputs)


def pair_up(core, own_ref, other_ref, out_ref):
    out_ref[core] = own_ref[...]
    out_ref[1 - core] = other_ref[...]


def pick_one(core, pair_ref, out_ref):
    out_ref[0] = pair_ref[core]


def line_up(core, *refs):
    *pair_refs, last_ref, out_ref = refs
    for i, ref in enumerate(pair_refs):
        out_ref[2 * i : 2 * i + 2] = ref[...]
    out_ref[2 * len(pair_refs)] = last_ref[0]


def put_together(core, *refs):
    for half in range(2):
        first, second, out = refs[half], refs[2 + half], refs[4 + half]
        size = first.shape[0]
        out[:size] = first[...]
        out[size:] = second[...]


def join(core, own, got):
    rows, units = own[0].shape
    return small_kernel(put_together, core, [(2 * rows, units)] * 2, *own, *got)


def wide(value):
    return value.astype(jnp.float32)


def first_sum(core, mine_ref, got_ref, near_ref, far_ref, out_ref):
    for i in range(2):
        out_ref[i] = (wide(mine_ref[i]) + wide(got_ref[i])).astype(jnp.bfloat16)
    total = wide(mine_ref[core]) + wide(got_ref[core]) + wide(near_ref[0]) + wide(far_ref[0])
    out_ref[core] = total.astype(jnp.bfloat16)


def second_sum(core, mine_ref, got_ref, arrived_ref, out_ref):
    for i in range(2):
        total = wide(mine_ref[2 + i]) + wide(got_ref[2 + i]) + wide(arrived_ref[i])
        out_ref[i] = total.astype(jnp.bfloat16)


def third_sum(core, mine_ref, got_ref, arrived_ref, keep_ref, give_ref):
    for which, out_ref in ((core, keep_ref), (1 - core, give_ref)):
        total = wide(mine_ref[4 + which]) + wide(got_ref[4 + which]) + wide(arrived_ref[which])
        out_ref[...] = total.astype(jnp.bfloat16)


def last_sum(core, mine_ref, got_ref, near_ref, far_ref, out_ref):
    total = wide(mine_ref[6]) + wide(got_ref[6]) + wide(near_ref[...]) + wide(far_ref[...])
    out_ref[...] = total.astype(jnp.bfloat16)


def partial_kernel(parts, sub, slot_ref, w_ref, *refs):
    *out_refs, result, out_sem = refs[-6:]
    for i, (first, half) in enumerate(parts):
        result[i] = lax.dot_general(
            refs[i][...], w_ref[...], (((1,), (1,)), ((), ())), preferred_element_type=jnp.float32
        ).astype(jnp.bfloat16)
        for p in range(PLACES):
            slot = slot_ref[half * ROWS + first + p]
            source = result.at[i, pl.ds(p * sub, sub), :]
            for out_ref, low, high in zip(out_refs, (0, 1, ZS, ZS + 1), (1, ZS, ZS + 1, 2 * ZS)):

                @pl.when((slot >= low) & (slot < high))
                def _():
                    pltpu.make_async_copy(
                        source, out_ref.at[slot - low, pl.ds(half * sub, sub), :], out_sem
                    ).start()

    pltpu.make_async_copy(result, result, out_sem).wait()


def partial_sums(slots, parts, pieces, weight, into=()):
    sub = pieces[0].shape[0] // PLACES
    features = weight.shape[0]
    count = len(pieces)
    anywhere, vmem = pl.BlockSpec(memory_space=pl.ANY), pl.BlockSpec(memory_space=pltpu.VMEM)
    inputs = (weight, *pieces, *into)
    return pl.pallas_call(
        lambda *refs: partial_kernel(parts, sub, *refs),
        out_shape=[
            jax.ShapeDtypeStruct((n, 2 * sub, features), jnp.bfloat16)
            for n in (1, ZS - 1, 1, ZS - 1)
        ],
        in_specs=[pl.BlockSpec(memory_space=pltpu.SMEM)]
        + [vmem] * (1 + count)
        + [anywhere] * len(into),
        out_specs=[anywhere] * 4,
        scratch_shapes=[
            pltpu.VMEM((count, PLACES * sub, features), jnp.bfloat16),
            pltpu.SemaphoreType.DMA,
        ],
        input_output_aliases={2 + count + i: i for i in range(len(into))},
        compiler_params=pltpu.CompilerParams(vmem_limit_bytes=10 * MIB),
        cost_estimate=COST,
        name="partial_sums",
    )(slots, *inputs)


def turn_kernel(place_ref, *refs):
    sources, (out_ref, ordered) = refs[:-2], refs[-2:]
    total = ordered.shape[0]
    sub = total // (2 * ROWS)
    index = 0
    for source in sources:
        for b in range(source.shape[0]):
            for half in range(2):
                row = pl.multiple_of(place_ref[index] * sub, sub)
                ordered[pl.ds(row, sub), :] = source[b, half * sub : (half + 1) * sub, :]
                index += 1
    features = ordered.shape[1]
    for at in range(0, features, WIDE):
        size = min(WIDE, features - at)
        place = lambda axis: lax.broadcasted_iota(jnp.int32, (size, size), axis)
        one = jnp.where(place(0) == place(1), 1.0, 0.0).astype(jnp.bfloat16)
        out_ref[at : at + size, :] = lax.dot_general(
            one,
            ordered[:, at : at + size],
            (((1,), (1,)), ((), ())),
            preferred_element_type=jnp.float32,
        ).astype(jnp.bfloat16)


def turned_tokens(places, sources):
    features = sources[0].shape[-1]
    total = sum(source.shape[0] * source.shape[1] for source in sources)
    return pl.pallas_call(
        turn_kernel,
        out_shape=jax.ShapeDtypeStruct((features, total), jnp.bfloat16),
        grid_spec=pltpu.PrefetchScalarGridSpec(
            num_scalar_prefetch=1,
            grid=(),
            in_specs=[pl.BlockSpec(memory_space=pltpu.VMEM)] * len(sources),
            out_specs=pl.BlockSpec(memory_space=pltpu.VMEM),
            scratch_shapes=[pltpu.VMEM((total, features), jnp.bfloat16)],
        ),
        compiler_params=pltpu.CompilerParams(vmem_limit_bytes=14 * MIB),
        cost_estimate=pl.CostEstimate(flops=0, bytes_accessed=16_000_000, transcendentals=0),
        name="turned_tokens",
    )(places, *sources)


def weight_kernel(count, turned_ref, *refs):
    pieces, out_ref = refs[:count], refs[-1]
    sums, at = None, 0
    for piece in pieces:
        rows = piece.shape[0]
        term = jnp.dot(
            turned_ref[:, at : at + rows], piece[...], preferred_element_type=jnp.float32
        )
        sums = term if sums is None else sums + term
        at += rows
    out_ref[...] = sums.astype(jnp.bfloat16)


def weight_gradient(turned, pieces, begin, end, into=None):
    features, total = turned.shape
    units = pieces[0].shape[1]
    inputs = (turned, *pieces) + (() if into is None else (into,))
    return pl.pallas_call(
        lambda *refs: weight_kernel(len(pieces), *refs),
        out_shape=jax.ShapeDtypeStruct((features, units), jnp.bfloat16),
        grid=(end - begin,),
        in_specs=[pl.BlockSpec(memory_space=pltpu.VMEM)]
        + [pl.BlockSpec((piece.shape[0], WIDE), lambda n: (0, n + begin)) for piece in pieces]
        + [pl.BlockSpec(memory_space=pl.ANY)] * (into is not None),
        out_specs=pl.BlockSpec((features, WIDE), lambda n: (0, n + begin)),
        input_output_aliases={} if into is None else {1 + len(pieces): 0},
        compiler_params=pltpu.CompilerParams(vmem_limit_bytes=16 * MIB),
        cost_estimate=pl.CostEstimate(
            flops=2 * total * WIDE * (end - begin) * features,
            bytes_accessed=2_000_000 * (end - begin),
            transcendentals=0,
        ),
        name="weight_gradient",
    )(*inputs)


def shards(tokens, cotangent, preact, weight):
    row, col = lax.axis_index("row"), lax.axis_index("col")
    z, core = col // 2, col % 2
    size, features = tokens.shape
    sub = size // 2
    table = held()
    block = row ^ jnp.asarray(table)[core]
    to, parity = (block // 2 - z) % ZS, block % 2
    worker = jnp.where(to % 4 == 0, parity, to // 4)
    away = jnp.where(to > 4, ZS - to, to)
    slot = jnp.where(away == 4, 0, jnp.where(away == 0, 7, 7 - 2 * away + parity))
    slots = jnp.where(worker == core, slot, slot + ZS).reshape(-1).astype(jnp.int32)
    down = 2 * core - 1
    chips = [z] + [z + down * i for i in (1, 2, 3)]
    blocks = [(p % ZS) * 2 + c for p in chips for c in range(2)] + [(z + 4) % ZS * 2 + core]
    chips = [z - down * i for i in (1, 2, 3)]
    blocks += [(p % ZS) * 2 + c for p in chips for c in range(2)] + [(z + 4) % ZS * 2 + 1 - core]
    place = jnp.asarray(places_of(table))[core][:, jnp.stack(blocks) ^ row]
    start = (place // PLACES * 2 + jnp.arange(2)[:, None]) * PLACES + place % PLACES
    starts = start.T.reshape(-1).astype(jnp.int32)

    partner = swap(tokens, "token_pair")
    core = core.reshape(1).astype(jnp.int32)
    own = []
    for half in range(2):
        rows = slice(half * sub, (half + 1) * sub)
        values, slope_at = cotangent[rows], preact[rows]
        if half:
            values, slope_at, *own = lax.optimization_barrier((values, slope_at, *own))
        own.append((values.astype(jnp.float32) * gelu_slope(slope_at)).astype(jnp.bfloat16))
    got = [across(own[half], half, 0) for half in range(2)]
    (chip,) = small_kernel(pair_up, core, [(2, size, features)], tokens, partner)
    first = [across(own[half], half, 1) for half in range(2)]
    ring = [onward(chip, "tokens1")]
    *got, chip, slots, starts = lax.optimization_barrier((*got, chip, slots, starts))
    second = [across(got[half], half, 1) for half in range(2)]
    own = join(core, own, got)
    early = [across(own[half], half, 2) for half in range(2)]
    first, second, ring[0] = lax.optimization_barrier((first, second, ring[0]))
    got = join(core, first, second)
    own = join(core, own, got)
    late = [across(got[half], half, 2) for half in range(2)]
    ring.append(onward(ring[0], "tokens2"))
    both_halves = lambda first: ((first, 0), (first, 1))
    own, early = lax.optimization_barrier((own, early))
    near = [across(own[half], half, 3) for half in range(2)]
    sums = partial_sums(slots, both_halves(0), own, weight)
    early, late, ring[1], sums = lax.optimization_barrier((early, late, ring[1], sums))
    got = join(core, early, late)
    far = [across(got[half], half, 3) for half in range(2)]
    ring.append(onward(ring[1], "tokens3"))
    sums = partial_sums(slots, both_halves(4), got, weight, into=sums)
    near, sums = lax.optimization_barrier((near, sums))
    sums = partial_sums(slots, both_halves(8), near, weight, into=sums)
    far[0], ring, sums = lax.optimization_barrier((far[0], ring, sums))
    ring.append(
        onward(small_kernel(pick_one, core, [(1, size, features)], ring[2])[0], "tokens4")
    )
    for half in range(2):
        far[half], sums = lax.optimization_barrier((far[half], sums))
        sums = partial_sums(slots, ((12, half),), far[half : half + 1], weight, into=sums)
    mine_far, mine, other_far, other = sums
    pieces = [*own, *got, *near, *far]

    near = onward(mine_far, "sums1")
    far = permute(other_far, lambda r, z, c: (r, z - 1 + 2 * c, 1 - c), "sums1x")
    got = swap(other, "sum_swap")
    near, far, got = lax.optimization_barrier((near, far, got))
    pair = (2, size, features)
    (running,) = small_kernel(first_sum, core, [pair], mine, got, near, far)
    arrived = onward(running, "sums2")
    ring, _ = lax.optimization_barrier((ring, running))
    (passed,) = small_kernel(line_up, core, [(7, size, features)], *ring)
    others = swap(passed, "token_swap")
    token_arrays, _ = lax.optimization_barrier(([chip, *ring, others], running))
    turned = turned_tokens(starts, token_arrays)
    arrived, turned = lax.optimization_barrier((arrived, turned))
    (running,) = small_kernel(second_sum, core, [pair], mine, got, arrived)
    arrived = onward(running, "sums3")
    turned, _ = lax.optimization_barrier((turned, running))
    tiles = pieces[0].shape[1] // WIDE
    part = tiles - tiles // 3
    weight_grad = weight_gradient(turned, pieces, 0, part)
    arrived, weight_grad, turned = lax.optimization_barrier((arrived, weight_grad, turned))
    keep, give = small_kernel(third_sum, core, [(size, features)] * 2, mine, got, arrived)
    near = onward(keep, "sums4")
    far = permute(give, lambda r, z, c: (r, z + 1 - 2 * c, 1 - c), "sums4x")
    turned, _ = lax.optimization_barrier((turned, keep))
    weight_grad = weight_gradient(turned, pieces, part, tiles, into=weight_grad)
    near, far, weight_grad = lax.optimization_barrier((near, far, weight_grad))
    (input_grad,) = small_kernel(last_sum, core, [(size, features)], mine, got, near, far)
    return input_grad, weight_grad


def solution(mesh):
    placed = (P("col", "row"), P("row", "col"), P("row", "col"), P("row", "col"))
    return jax.shard_map(
        shards,
        mesh=mesh,
        in_specs=placed,
        out_specs=(P("col", "row"), P("row", "col")),
        check_vma=False,
    )
```

```python
import jax
import jax.numpy as jnp
import numpy as np
from jax import lax
from jax.experimental import pallas as pl
from jax.experimental.pallas import tpu as pltpu
from jax.sharding import PartitionSpec as P

root_two_over_pi = 0.7978845608
cubic_coef = 0.044715

ROWS, ZS = 16, 8
ORDER = (
    ((4, 12, 1, 3), (1, 3, 4, 12)),
    ((12, 4, 3, 1), (3, 1, 12, 4)),
)
PLACES, WIDE = 4, 256
MIB = 1024 * 1024
COST = pl.CostEstimate(flops=1_000_000, bytes_accessed=1_000_000, transcendentals=0)


def held():
    table = np.zeros((2, 2, ROWS), np.int32)
    for core in range(2):
        for half in range(2):
            for place in range(ROWS):
                for step in range(4):
                    if place >> step & 1:
                        table[core, half, place] ^= ORDER[core][half][step]
    return table


def places_of(table):
    return np.argsort(table, axis=-1).astype(np.int32)


def permute(value, target, name):
    pairs = []
    for row in range(ROWS):
        for col in range(2 * ZS):
            r, z, c = target(row, col // 2, col % 2)
            pairs.append((row * 2 * ZS + col, r * 2 * ZS + (z % ZS) * 2 + c))
    with jax.named_scope(name):
        return lax.ppermute(value, ("row", "col"), pairs)


def gelu_slope(preact):
    values = preact.astype(jnp.float32)
    hyper = jnp.tanh(root_two_over_pi * (values + cubic_coef * values * values * values))
    return 0.5 * (1.0 + hyper) + 0.5 * values * (1.0 - hyper * hyper) * root_two_over_pi * (
        1.0 + 3.0 * cubic_coef * values * values
    )


def across(value, half, step):
    return permute(value, lambda r, z, c: (r ^ ORDER[c][half][step], z, c), f"x{step}{half}")


def onward(value, name):
    return permute(value, lambda r, z, c: (r, z + 1 - 2 * c, c), name)


def swap(value, name):
    return permute(value, lambda r, z, c: (r, z, 1 - c), name)


def small_kernel(kernel, core, outs, *inputs):
    vmem = pl.BlockSpec(memory_space=pltpu.VMEM)
    return pl.pallas_call(
        lambda core_ref, *refs: kernel(core_ref[0], *refs),
        out_shape=[jax.ShapeDtypeStruct(shape, jnp.bfloat16) for shape in outs],
        in_specs=[pl.BlockSpec(memory_space=pltpu.SMEM)] + [vmem] * len(inputs),
        out_specs=[vmem] * len(outs),
        compiler_params=pltpu.CompilerParams(vmem_limit_bytes=6 * MIB),
        cost_estimate=COST,
        name=kernel.__name__.strip("_"),
    )(core, *inputs)


def pair_up(core, own_ref, other_ref, out_ref):
    out_ref[core] = own_ref[...]
    out_ref[1 - core] = other_ref[...]


def pick_one(core, pair_ref, out_ref):
    out_ref[0] = pair_ref[core]


def line_up(core, first_ref, second_ref, third_ref, out_ref):
    for i, ref in enumerate((first_ref, second_ref, third_ref)):
        out_ref[2 * i : 2 * i + 2] = ref[...]


def put_together(core, *refs):
    for half in range(2):
        first, second, out = refs[half], refs[2 + half], refs[4 + half]
        size = first.shape[0]
        out[:size] = first[...]
        out[size:] = second[...]


def join(core, own, got):
    rows, units = own[0].shape
    return small_kernel(put_together, core, [(2 * rows, units)] * 2, *own, *got)


def wide(value):
    return value.astype(jnp.float32)


def first_sum(core, mine_ref, got_ref, near_ref, far_ref, out_ref):
    for i in range(2):
        out_ref[i] = (wide(mine_ref[i]) + wide(got_ref[i])).astype(jnp.bfloat16)
    total = wide(mine_ref[core]) + wide(got_ref[core]) + wide(near_ref[0]) + wide(far_ref[0])
    out_ref[core] = total.astype(jnp.bfloat16)


def second_sum(core, mine_ref, got_ref, arrived_ref, out_ref):
    for i in range(2):
        total = wide(mine_ref[2 + i]) + wide(got_ref[2 + i]) + wide(arrived_ref[i])
        out_ref[i] = total.astype(jnp.bfloat16)


def third_sum(core, mine_ref, got_ref, arrived_ref, keep_ref, give_ref):
    for which, out_ref in ((core, keep_ref), (1 - core, give_ref)):
        total = wide(mine_ref[4 + which]) + wide(got_ref[4 + which]) + wide(arrived_ref[which])
        out_ref[...] = total.astype(jnp.bfloat16)


def last_sum(core, mine_ref, got_ref, near_ref, far_ref, out_ref):
    total = wide(mine_ref[6]) + wide(got_ref[6]) + wide(near_ref[...]) + wide(far_ref[...])
    out_ref[...] = total.astype(jnp.bfloat16)


def partial_kernel(parts, sub, slot_ref, w_ref, *refs):
    *out_refs, result, out_sem = refs[-6:]
    for i, (first, half) in enumerate(parts):
        result[i] = lax.dot_general(
            refs[i][...], w_ref[...], (((1,), (1,)), ((), ())), preferred_element_type=jnp.float32
        ).astype(jnp.bfloat16)
        for p in range(PLACES):
            slot = slot_ref[half * ROWS + first + p]
            source = result.at[i, pl.ds(p * sub, sub), :]
            for out_ref, low, high in zip(out_refs, (0, 1, ZS, ZS + 1), (1, ZS, ZS + 1, 2 * ZS)):

                @pl.when((slot >= low) & (slot < high))
                def _():
                    pltpu.make_async_copy(
                        source, out_ref.at[slot - low, pl.ds(half * sub, sub), :], out_sem
                    ).start()

    pltpu.make_async_copy(result, result, out_sem).wait()


def partial_sums(slots, parts, pieces, weight, into=()):
    sub = pieces[0].shape[0] // PLACES
    features = weight.shape[0]
    count = len(pieces)
    anywhere, vmem = pl.BlockSpec(memory_space=pl.ANY), pl.BlockSpec(memory_space=pltpu.VMEM)
    inputs = (weight, *pieces, *into)
    return pl.pallas_call(
        lambda *refs: partial_kernel(parts, sub, *refs),
        out_shape=[
            jax.ShapeDtypeStruct((n, 2 * sub, features), jnp.bfloat16)
            for n in (1, ZS - 1, 1, ZS - 1)
        ],
        in_specs=[pl.BlockSpec(memory_space=pltpu.SMEM)]
        + [vmem] * (1 + count)
        + [anywhere] * len(into),
        out_specs=[anywhere] * 4,
        scratch_shapes=[
            pltpu.VMEM((count, PLACES * sub, features), jnp.bfloat16),
            pltpu.SemaphoreType.DMA,
        ],
        input_output_aliases={2 + count + i: i for i in range(len(into))},
        compiler_params=pltpu.CompilerParams(vmem_limit_bytes=10 * MIB),
        cost_estimate=COST,
        name="partial_sums",
    )(slots, *inputs)


def turn_kernel(place_ref, *refs):
    sources, (out_ref, ordered) = refs[:-2], refs[-2:]
    total = ordered.shape[0]
    sub = total // (2 * ROWS)
    index = 0
    for source in sources:
        for b in range(source.shape[0]):
            for half in range(2):
                row = pl.multiple_of(place_ref[index] * sub, sub)
                ordered[pl.ds(row, sub), :] = source[b, half * sub : (half + 1) * sub, :]
                index += 1
    features = ordered.shape[1]
    for at in range(0, features, WIDE):
        size = min(WIDE, features - at)
        place = lambda axis: lax.broadcasted_iota(jnp.int32, (size, size), axis)
        one = jnp.where(place(0) == place(1), 1.0, 0.0).astype(jnp.bfloat16)
        out_ref[at : at + size, :] = lax.dot_general(
            one,
            ordered[:, at : at + size],
            (((1,), (1,)), ((), ())),
            preferred_element_type=jnp.float32,
        ).astype(jnp.bfloat16)


def turned_tokens(places, sources):
    features = sources[0].shape[-1]
    total = sum(source.shape[0] * source.shape[1] for source in sources)
    return pl.pallas_call(
        turn_kernel,
        out_shape=jax.ShapeDtypeStruct((features, total), jnp.bfloat16),
        grid_spec=pltpu.PrefetchScalarGridSpec(
            num_scalar_prefetch=1,
            grid=(),
            in_specs=[pl.BlockSpec(memory_space=pltpu.VMEM)] * len(sources),
            out_specs=pl.BlockSpec(memory_space=pltpu.VMEM),
            scratch_shapes=[pltpu.VMEM((total, features), jnp.bfloat16)],
        ),
        compiler_params=pltpu.CompilerParams(vmem_limit_bytes=14 * MIB),
        cost_estimate=pl.CostEstimate(flops=0, bytes_accessed=16_000_000, transcendentals=0),
        name="turned_tokens",
    )(places, *sources)


def weight_kernel(count, turned_ref, *refs):
    pieces, out_ref = refs[:count], refs[-1]
    sums, at = None, 0
    for piece in pieces:
        rows = piece.shape[0]
        term = jnp.dot(
            turned_ref[:, at : at + rows], piece[...], preferred_element_type=jnp.float32
        )
        sums = term if sums is None else sums + term
        at += rows
    out_ref[...] = sums.astype(jnp.bfloat16)


def weight_gradient(turned, pieces, begin, end, into=None):
    features, total = turned.shape
    units = pieces[0].shape[1]
    inputs = (turned, *pieces) + (() if into is None else (into,))
    return pl.pallas_call(
        lambda *refs: weight_kernel(len(pieces), *refs),
        out_shape=jax.ShapeDtypeStruct((features, units), jnp.bfloat16),
        grid=(end - begin,),
        in_specs=[pl.BlockSpec(memory_space=pltpu.VMEM)]
        + [pl.BlockSpec((piece.shape[0], WIDE), lambda n: (0, n + begin)) for piece in pieces]
        + [pl.BlockSpec(memory_space=pl.ANY)] * (into is not None),
        out_specs=pl.BlockSpec((features, WIDE), lambda n: (0, n + begin)),
        input_output_aliases={} if into is None else {1 + len(pieces): 0},
        compiler_params=pltpu.CompilerParams(vmem_limit_bytes=16 * MIB),
        cost_estimate=pl.CostEstimate(
            flops=2 * total * WIDE * (end - begin) * features,
            bytes_accessed=2_000_000 * (end - begin),
            transcendentals=0,
        ),
        name="weight_gradient",
    )(*inputs)


def shards(tokens, cotangent, preact, weight):
    row, col = lax.axis_index("row"), lax.axis_index("col")
    z, core = col // 2, col % 2
    size, features = tokens.shape
    sub = size // 2
    table = held()
    block = row ^ jnp.asarray(table)[core]
    to, parity = (block // 2 - z) % ZS, block % 2
    worker = jnp.where(to % 4 == 0, parity, to // 4)
    away = jnp.where(to > 4, ZS - to, to)
    slot = jnp.where(away == 4, 0, jnp.where(away == 0, 7, 7 - 2 * away + parity))
    slots = jnp.where(worker == core, slot, slot + ZS).reshape(-1).astype(jnp.int32)
    down = 2 * core - 1
    chips = [z] + [z + down * i for i in (1, 2, 3)]
    blocks = [(p % ZS) * 2 + c for p in chips for c in range(2)] + [(z + 4) % ZS * 2 + core]
    chips = [z - down * i for i in (1, 2, 3)]
    blocks += [(p % ZS) * 2 + c for p in chips for c in range(2)] + [(z + 4) % ZS * 2 + 1 - core]
    place = jnp.asarray(places_of(table))[core][:, jnp.stack(blocks) ^ row]
    start = (place // PLACES * 2 + jnp.arange(2)[:, None]) * PLACES + place % PLACES
    starts = start.T.reshape(-1).astype(jnp.int32)

    partner = swap(tokens, "token_pair")
    core = core.reshape(1).astype(jnp.int32)
    own = []
    for half in range(2):
        rows = slice(half * sub, (half + 1) * sub)
        values, slope_at = cotangent[rows], preact[rows]
        if half:
            values, slope_at, *own = lax.optimization_barrier((values, slope_at, *own))
        own.append((values.astype(jnp.float32) * gelu_slope(slope_at)).astype(jnp.bfloat16))
    got = [across(own[half], half, 0) for half in range(2)]
    (chip,) = small_kernel(pair_up, core, [(2, size, features)], tokens, partner)
    first = [across(own[half], half, 1) for half in range(2)]
    ring = [onward(chip, "tokens1")]
    *got, chip, slots, starts = lax.optimization_barrier((*got, chip, slots, starts))
    second = [across(got[half], half, 1) for half in range(2)]
    own = join(core, own, got)
    early = [across(own[half], half, 2) for half in range(2)]
    first, second, ring[0] = lax.optimization_barrier((first, second, ring[0]))
    got = join(core, first, second)
    own = join(core, own, got)
    late = [across(got[half], half, 2) for half in range(2)]
    ring.append(onward(ring[0], "tokens2"))
    both_halves = lambda first: ((first, 0), (first, 1))
    own, early = lax.optimization_barrier((own, early))
    near = [across(own[half], half, 3) for half in range(2)]
    sums = partial_sums(slots, both_halves(0), own, weight)
    early, late, ring[1], sums = lax.optimization_barrier((early, late, ring[1], sums))
    got = join(core, early, late)
    far = [across(got[half], half, 3) for half in range(2)]
    ring.append(onward(ring[1], "tokens3"))
    sums = partial_sums(slots, both_halves(4), got, weight, into=sums)
    near, sums = lax.optimization_barrier((near, sums))
    sums = partial_sums(slots, both_halves(8), near, weight, into=sums)
    far[0], ring, sums = lax.optimization_barrier((far[0], ring, sums))
    ring.append(
        onward(small_kernel(pick_one, core, [(1, size, features)], ring[2])[0], "tokens4")
    )
    for half in range(2):
        far[half], sums = lax.optimization_barrier((far[half], sums))
        sums = partial_sums(slots, ((12, half),), far[half : half + 1], weight, into=sums)
    mine_far, mine, other_far, other = sums
    pieces = [*own, *got, *near, *far]

    near = onward(mine_far, "sums1")
    far = permute(other_far, lambda r, z, c: (r, z - 1 + 2 * c, 1 - c), "sums1x")
    got = swap(other, "sum_swap")
    (passed,) = small_kernel(line_up, core, [(6, size, features)], *ring[:3])
    others = [swap(passed, "token_swap")]
    near, far, got, others = lax.optimization_barrier((near, far, got, others))
    pair = (2, size, features)
    (running,) = small_kernel(first_sum, core, [pair], mine, got, near, far)
    arrived = onward(running, "sums2")
    others.append(swap(ring[3], "last_swap"))
    token_arrays, _ = lax.optimization_barrier(([chip, *ring, *others], running))
    turned = turned_tokens(starts, token_arrays)
    arrived, turned = lax.optimization_barrier((arrived, turned))
    (running,) = small_kernel(second_sum, core, [pair], mine, got, arrived)
    arrived = onward(running, "sums3")
    turned, _ = lax.optimization_barrier((turned, running))
    tiles = pieces[0].shape[1] // WIDE
    part = tiles - tiles // 3
    weight_grad = weight_gradient(turned, pieces, 0, part)
    arrived, weight_grad, turned = lax.optimization_barrier((arrived, weight_grad, turned))
    keep, give = small_kernel(third_sum, core, [(size, features)] * 2, mine, got, arrived)
    near = onward(keep, "sums4")
    far = permute(give, lambda r, z, c: (r, z + 1 - 2 * c, 1 - c), "sums4x")
    turned, _ = lax.optimization_barrier((turned, keep))
    weight_grad = weight_gradient(turned, pieces, part, tiles, into=weight_grad)
    near, far, weight_grad = lax.optimization_barrier((near, far, weight_grad))
    (input_grad,) = small_kernel(last_sum, core, [(size, features)], mine, got, near, far)
    return input_grad, weight_grad


def solution(mesh):
    placed = (P("col", "row"), P("row", "col"), P("row", "col"), P("row", "col"))
    return jax.shard_map(
        shards,
        mesh=mesh,
        in_specs=placed,
        out_specs=(P("col", "row"), P("row", "col")),
        check_vma=False,
    )
```

```python
import jax
import jax.numpy as jnp
import numpy as np
from jax import lax
from jax.experimental import pallas as pl
from jax.experimental.pallas import tpu as pltpu
from jax.sharding import PartitionSpec as P

root_two_over_pi = 0.7978845608
cubic_coef = 0.044715

ROWS, ZS = 16, 8
ORDER = (
    ((4, 12, 1, 3), (1, 3, 4, 12)),
    ((12, 4, 3, 1), (3, 1, 12, 4)),
)
PLACES, WIDE = 4, 256
MIB = 1024 * 1024
COST = pl.CostEstimate(flops=1_000_000, bytes_accessed=1_000_000, transcendentals=0)


def held():
    table = np.zeros((2, 2, ROWS), np.int32)
    for core in range(2):
        for half in range(2):
            for place in range(ROWS):
                for step in range(4):
                    if place >> step & 1:
                        table[core, half, place] ^= ORDER[core][half][step]
    return table


def places_of(table):
    return np.argsort(table, axis=-1).astype(np.int32)


def permute(value, target, name):
    pairs = []
    for row in range(ROWS):
        for col in range(2 * ZS):
            r, z, c = target(row, col // 2, col % 2)
            pairs.append((row * 2 * ZS + col, r * 2 * ZS + (z % ZS) * 2 + c))
    with jax.named_scope(name):
        return lax.ppermute(value, ("row", "col"), pairs)


def gelu_slope(preact):
    values = preact.astype(jnp.float32)
    hyper = jnp.tanh(root_two_over_pi * (values + cubic_coef * values * values * values))
    return 0.5 * (1.0 + hyper) + 0.5 * values * (1.0 - hyper * hyper) * root_two_over_pi * (
        1.0 + 3.0 * cubic_coef * values * values
    )


def across(value, half, step):
    return permute(value, lambda r, z, c: (r ^ ORDER[c][half][step], z, c), f"x{step}{half}")


def onward(value, name):
    return permute(value, lambda r, z, c: (r, z + 1 - 2 * c, c), name)


def swap(value, name):
    return permute(value, lambda r, z, c: (r, z, 1 - c), name)


def small_kernel(kernel, core, outs, *inputs):
    vmem = pl.BlockSpec(memory_space=pltpu.VMEM)
    return pl.pallas_call(
        lambda core_ref, *refs: kernel(core_ref[0], *refs),
        out_shape=[jax.ShapeDtypeStruct(shape, jnp.bfloat16) for shape in outs],
        in_specs=[pl.BlockSpec(memory_space=pltpu.SMEM)] + [vmem] * len(inputs),
        out_specs=[vmem] * len(outs),
        compiler_params=pltpu.CompilerParams(vmem_limit_bytes=6 * MIB),
        cost_estimate=COST,
        name=kernel.__name__.strip("_"),
    )(core, *inputs)


def pair_up(core, own_ref, other_ref, out_ref):
    out_ref[core] = own_ref[...]
    out_ref[1 - core] = other_ref[...]


def pick_one(core, pair_ref, out_ref):
    out_ref[0] = pair_ref[core]


def line_up(core, first_ref, second_ref, third_ref, out_ref):
    for i, ref in enumerate((first_ref, second_ref, third_ref)):
        out_ref[2 * i : 2 * i + 2] = ref[...]


def put_together(core, *refs):
    for half in range(2):
        first, second, out = refs[half], refs[2 + half], refs[4 + half]
        size = first.shape[0]
        out[:size] = first[...]
        out[size:] = second[...]


def join(core, own, got):
    rows, units = own[0].shape
    return small_kernel(put_together, core, [(2 * rows, units)] * 2, *own, *got)


def wide(value):
    return value.astype(jnp.float32)


def first_sum(core, mine_ref, got_ref, near_ref, far_ref, out_ref):
    for i in range(2):
        out_ref[i] = (wide(mine_ref[i]) + wide(got_ref[i])).astype(jnp.bfloat16)
    total = wide(mine_ref[core]) + wide(got_ref[core]) + wide(near_ref[0]) + wide(far_ref[0])
    out_ref[core] = total.astype(jnp.bfloat16)


def second_sum(core, mine_ref, got_ref, arrived_ref, out_ref):
    for i in range(2):
        total = wide(mine_ref[2 + i]) + wide(got_ref[2 + i]) + wide(arrived_ref[i])
        out_ref[i] = total.astype(jnp.bfloat16)


def third_sum(core, mine_ref, got_ref, arrived_ref, keep_ref, give_ref):
    for which, out_ref in ((core, keep_ref), (1 - core, give_ref)):
        total = wide(mine_ref[4 + which]) + wide(got_ref[4 + which]) + wide(arrived_ref[which])
        out_ref[...] = total.astype(jnp.bfloat16)


def last_sum(core, mine_ref, got_ref, near_ref, far_ref, out_ref):
    total = wide(mine_ref[6]) + wide(got_ref[6]) + wide(near_ref[...]) + wide(far_ref[...])
    out_ref[...] = total.astype(jnp.bfloat16)


def partial_kernel(parts, sub, slot_ref, w_ref, *refs):
    *out_refs, result, out_sem = refs[-6:]
    features = w_ref.shape[0]
    for i, (first, half) in enumerate(parts):
        for low_column, high_column in ((0, 2 * WIDE), (2 * WIDE, features)):
            columns = slice(low_column, high_column)
            result[i, :, columns] = lax.dot_general(
                refs[i][...],
                w_ref[columns, :],
                (((1,), (1,)), ((), ())),
                preferred_element_type=jnp.float32,
            ).astype(jnp.bfloat16)
            for p in range(PLACES):
                slot = slot_ref[half * ROWS + first + p]
                source = result.at[i, pl.ds(p * sub, sub), columns]
                for out_ref, low, high in zip(
                    out_refs, (0, 1, ZS, ZS + 1), (1, ZS, ZS + 1, 2 * ZS)
                ):

                    @pl.when((slot >= low) & (slot < high))
                    def _():
                        pltpu.make_async_copy(
                            source,
                            out_ref.at[slot - low, pl.ds(half * sub, sub), columns],
                            out_sem,
                        ).start()

    pltpu.make_async_copy(result, result, out_sem).wait()


def partial_sums(slots, parts, pieces, weight, into=()):
    sub = pieces[0].shape[0] // PLACES
    features = weight.shape[0]
    count = len(pieces)
    anywhere, vmem = pl.BlockSpec(memory_space=pl.ANY), pl.BlockSpec(memory_space=pltpu.VMEM)
    inputs = (weight, *pieces, *into)
    return pl.pallas_call(
        lambda *refs: partial_kernel(parts, sub, *refs),
        out_shape=[
            jax.ShapeDtypeStruct((n, 2 * sub, features), jnp.bfloat16)
            for n in (1, ZS - 1, 1, ZS - 1)
        ],
        in_specs=[pl.BlockSpec(memory_space=pltpu.SMEM)]
        + [vmem] * (1 + count)
        + [anywhere] * len(into),
        out_specs=[anywhere] * 4,
        scratch_shapes=[
            pltpu.VMEM((count, PLACES * sub, features), jnp.bfloat16),
            pltpu.SemaphoreType.DMA,
        ],
        input_output_aliases={2 + count + i: i for i in range(len(into))},
        compiler_params=pltpu.CompilerParams(vmem_limit_bytes=10 * MIB),
        cost_estimate=COST,
        name="partial_sums",
    )(slots, *inputs)


def turn_kernel(place_ref, *refs):
    sources, (out_ref, ordered) = refs[:-2], refs[-2:]
    total = ordered.shape[0]
    sub = total // (2 * ROWS)
    index = 0
    for source in sources:
        for b in range(source.shape[0]):
            for half in range(2):
                row = pl.multiple_of(place_ref[index] * sub, sub)
                ordered[pl.ds(row, sub), :] = source[b, half * sub : (half + 1) * sub, :]
                index += 1
    features = ordered.shape[1]
    for at in range(0, features, WIDE):
        size = min(WIDE, features - at)
        place = lambda axis: lax.broadcasted_iota(jnp.int32, (size, size), axis)
        one = jnp.where(place(0) == place(1), 1.0, 0.0).astype(jnp.bfloat16)
        out_ref[at : at + size, :] = lax.dot_general(
            one,
            ordered[:, at : at + size],
            (((1,), (1,)), ((), ())),
            preferred_element_type=jnp.float32,
        ).astype(jnp.bfloat16)


def turned_tokens(places, sources):
    features = sources[0].shape[-1]
    total = sum(source.shape[0] * source.shape[1] for source in sources)
    return pl.pallas_call(
        turn_kernel,
        out_shape=jax.ShapeDtypeStruct((features, total), jnp.bfloat16),
        grid_spec=pltpu.PrefetchScalarGridSpec(
            num_scalar_prefetch=1,
            grid=(),
            in_specs=[pl.BlockSpec(memory_space=pltpu.VMEM)] * len(sources),
            out_specs=pl.BlockSpec(memory_space=pltpu.VMEM),
            scratch_shapes=[pltpu.VMEM((total, features), jnp.bfloat16)],
        ),
        compiler_params=pltpu.CompilerParams(vmem_limit_bytes=14 * MIB),
        cost_estimate=pl.CostEstimate(flops=0, bytes_accessed=16_000_000, transcendentals=0),
        name="turned_tokens",
    )(places, *sources)


def weight_kernel(count, turned_ref, *refs):
    pieces, out_ref = refs[:count], refs[-1]
    sums, at = None, 0
    for piece in pieces:
        rows = piece.shape[0]
        term = jnp.dot(
            turned_ref[:, at : at + rows], piece[...], preferred_element_type=jnp.float32
        )
        sums = term if sums is None else sums + term
        at += rows
    out_ref[...] = sums.astype(jnp.bfloat16)


def weight_gradient(turned, pieces, begin, end, into=None):
    features, total = turned.shape
    units = pieces[0].shape[1]
    inputs = (turned, *pieces) + (() if into is None else (into,))
    return pl.pallas_call(
        lambda *refs: weight_kernel(len(pieces), *refs),
        out_shape=jax.ShapeDtypeStruct((features, units), jnp.bfloat16),
        grid=(end - begin,),
        in_specs=[pl.BlockSpec(memory_space=pltpu.VMEM)]
        + [pl.BlockSpec((piece.shape[0], WIDE), lambda n: (0, n + begin)) for piece in pieces]
        + [pl.BlockSpec(memory_space=pl.ANY)] * (into is not None),
        out_specs=pl.BlockSpec((features, WIDE), lambda n: (0, n + begin)),
        input_output_aliases={} if into is None else {1 + len(pieces): 0},
        compiler_params=pltpu.CompilerParams(vmem_limit_bytes=16 * MIB),
        cost_estimate=pl.CostEstimate(
            flops=2 * total * WIDE * (end - begin) * features,
            bytes_accessed=2_000_000 * (end - begin),
            transcendentals=0,
        ),
        name="weight_gradient",
    )(*inputs)


def shards(tokens, cotangent, preact, weight):
    row, col = lax.axis_index("row"), lax.axis_index("col")
    z, core = col // 2, col % 2
    size, features = tokens.shape
    sub = size // 2
    table = held()
    block = row ^ jnp.asarray(table)[core]
    to, parity = (block // 2 - z) % ZS, block % 2
    worker = jnp.where(to % 4 == 0, parity, to // 4)
    away = jnp.where(to > 4, ZS - to, to)
    slot = jnp.where(away == 4, 0, jnp.where(away == 0, 7, 7 - 2 * away + parity))
    slots = jnp.where(worker == core, slot, slot + ZS).reshape(-1).astype(jnp.int32)
    down = 2 * core - 1
    chips = [z] + [z + down * i for i in (1, 2, 3)]
    blocks = [(p % ZS) * 2 + c for p in chips for c in range(2)] + [(z + 4) % ZS * 2 + core]
    chips = [z - down * i for i in (1, 2, 3)]
    blocks += [(p % ZS) * 2 + c for p in chips for c in range(2)] + [(z + 4) % ZS * 2 + 1 - core]
    place = jnp.asarray(places_of(table))[core][:, jnp.stack(blocks) ^ row]
    start = (place // PLACES * 2 + jnp.arange(2)[:, None]) * PLACES + place % PLACES
    starts = start.T.reshape(-1).astype(jnp.int32)

    partner = swap(tokens, "token_pair")
    core = core.reshape(1).astype(jnp.int32)
    own = []
    for half in range(2):
        rows = slice(half * sub, (half + 1) * sub)
        values, slope_at = cotangent[rows], preact[rows]
        if half:
            values, slope_at, *own = lax.optimization_barrier((values, slope_at, *own))
        own.append((values.astype(jnp.float32) * gelu_slope(slope_at)).astype(jnp.bfloat16))
    got = [across(own[half], half, 0) for half in range(2)]
    (chip,) = small_kernel(pair_up, core, [(2, size, features)], tokens, partner)
    first = [across(own[half], half, 1) for half in range(2)]
    ring = [onward(chip, "tokens1")]
    *got, chip, slots, starts = lax.optimization_barrier((*got, chip, slots, starts))
    second = [across(got[half], half, 1) for half in range(2)]
    own = join(core, own, got)
    early = [across(own[half], half, 2) for half in range(2)]
    first, second, ring[0] = lax.optimization_barrier((first, second, ring[0]))
    got = join(core, first, second)
    own = join(core, own, got)
    late = [across(got[half], half, 2) for half in range(2)]
    ring.append(onward(ring[0], "tokens2"))
    both_halves = lambda first: ((first, 0), (first, 1))
    own, early = lax.optimization_barrier((own, early))
    near = [across(own[half], half, 3) for half in range(2)]
    sums = partial_sums(slots, both_halves(0), own, weight)
    early, late, ring[1], sums = lax.optimization_barrier((early, late, ring[1], sums))
    got = join(core, early, late)
    far = [across(got[half], half, 3) for half in range(2)]
    ring.append(onward(ring[1], "tokens3"))
    sums = partial_sums(slots, both_halves(4), got, weight, into=sums)
    near, sums = lax.optimization_barrier((near, sums))
    sums = partial_sums(slots, both_halves(8), near, weight, into=sums)
    far[0], ring, sums = lax.optimization_barrier((far[0], ring, sums))
    ring.append(
        onward(small_kernel(pick_one, core, [(1, size, features)], ring[2])[0], "tokens4")
    )
    for half in range(2):
        far[half], sums = lax.optimization_barrier((far[half], sums))
        sums = partial_sums(slots, ((12, half),), far[half : half + 1], weight, into=sums)
    mine_far, mine, other_far, other = sums
    pieces = [*own, *got, *near, *far]

    near = onward(mine_far, "sums1")
    far = permute(other_far, lambda r, z, c: (r, z - 1 + 2 * c, 1 - c), "sums1x")
    got = swap(other, "sum_swap")
    (passed,) = small_kernel(line_up, core, [(6, size, features)], *ring[:3])
    others = [swap(passed, "token_swap")]
    near, far, got, others = lax.optimization_barrier((near, far, got, others))
    pair = (2, size, features)
    (running,) = small_kernel(first_sum, core, [pair], mine, got, near, far)
    arrived = onward(running, "sums2")
    others.append(swap(ring[3], "last_swap"))
    token_arrays, _ = lax.optimization_barrier(([chip, *ring, *others], running))
    turned = turned_tokens(starts, token_arrays)
    arrived, turned = lax.optimization_barrier((arrived, turned))
    (running,) = small_kernel(second_sum, core, [pair], mine, got, arrived)
    arrived = onward(running, "sums3")
    turned, _ = lax.optimization_barrier((turned, running))
    tiles = pieces[0].shape[1] // WIDE
    part = tiles - tiles // 3
    weight_grad = weight_gradient(turned, pieces, 0, part)
    arrived, weight_grad, turned = lax.optimization_barrier((arrived, weight_grad, turned))
    keep, give = small_kernel(third_sum, core, [(size, features)] * 2, mine, got, arrived)
    near = onward(keep, "sums4")
    far = permute(give, lambda r, z, c: (r, z + 1 - 2 * c, 1 - c), "sums4x")
    turned, _ = lax.optimization_barrier((turned, keep))
    weight_grad = weight_gradient(turned, pieces, part, tiles, into=weight_grad)
    near, far, weight_grad = lax.optimization_barrier((near, far, weight_grad))
    (input_grad,) = small_kernel(last_sum, core, [(size, features)], mine, got, near, far)
    return input_grad, weight_grad


def solution(mesh):
    placed = (P("col", "row"), P("row", "col"), P("row", "col"), P("row", "col"))
    return jax.shard_map(
        shards,
        mesh=mesh,
        in_specs=placed,
        out_specs=(P("col", "row"), P("row", "col")),
        check_vma=False,
    )
```

```python
import jax
import jax.numpy as jnp
import numpy as np
from jax import lax
from jax.experimental import pallas as pl
from jax.experimental.pallas import tpu as pltpu
from jax.sharding import PartitionSpec as P

root_two_over_pi = 0.7978845608
cubic_coef = 0.044715

ROWS, ZS = 16, 8
ORDER = (
    ((4, 12, 1, 3), (1, 3, 4, 12)),
    ((12, 4, 3, 1), (3, 1, 12, 4)),
)
PLACES, WIDE = 4, 256
MIB = 1024 * 1024
COST = pl.CostEstimate(flops=1_000_000, bytes_accessed=1_000_000, transcendentals=0)


def held():
    table = np.zeros((2, 2, ROWS), np.int32)
    for core in range(2):
        for half in range(2):
            for place in range(ROWS):
                for step in range(4):
                    if place >> step & 1:
                        table[core, half, place] ^= ORDER[core][half][step]
    return table


def places_of(table):
    return np.argsort(table, axis=-1).astype(np.int32)


def permute(value, target, name):
    pairs = []
    for row in range(ROWS):
        for col in range(2 * ZS):
            r, z, c = target(row, col // 2, col % 2)
            pairs.append((row * 2 * ZS + col, r * 2 * ZS + (z % ZS) * 2 + c))
    with jax.named_scope(name):
        return lax.ppermute(value, ("row", "col"), pairs)


def gelu_slope(preact):
    values = preact.astype(jnp.float32)
    hyper = jnp.tanh(root_two_over_pi * (values + cubic_coef * values * values * values))
    return 0.5 * (1.0 + hyper) + 0.5 * values * (1.0 - hyper * hyper) * root_two_over_pi * (
        1.0 + 3.0 * cubic_coef * values * values
    )


def across(value, half, step):
    return permute(value, lambda r, z, c: (r ^ ORDER[c][half][step], z, c), f"x{step}{half}")


def onward(value, name):
    return permute(value, lambda r, z, c: (r, z + 1 - 2 * c, c), name)


def swap(value, name):
    return permute(value, lambda r, z, c: (r, z, 1 - c), name)


def small_kernel(kernel, core, outs, *inputs):
    vmem = pl.BlockSpec(memory_space=pltpu.VMEM)
    return pl.pallas_call(
        lambda core_ref, *refs: kernel(core_ref[0], *refs),
        out_shape=[jax.ShapeDtypeStruct(shape, jnp.bfloat16) for shape in outs],
        in_specs=[pl.BlockSpec(memory_space=pltpu.SMEM)] + [vmem] * len(inputs),
        out_specs=[vmem] * len(outs),
        compiler_params=pltpu.CompilerParams(vmem_limit_bytes=6 * MIB),
        cost_estimate=COST,
        name=kernel.__name__.strip("_"),
    )(core, *inputs)


def pair_up(core, own_ref, other_ref, out_ref):
    out_ref[core] = own_ref[...]
    out_ref[1 - core] = other_ref[...]


def pick_one(core, pair_ref, out_ref):
    out_ref[0] = pair_ref[core]


def line_up(core, first_ref, second_ref, third_ref, out_ref):
    for i, ref in enumerate((first_ref, second_ref, third_ref)):
        out_ref[2 * i : 2 * i + 2] = ref[...]


def put_together(core, *refs):
    for half in range(2):
        first, second, out = refs[half], refs[2 + half], refs[4 + half]
        size = first.shape[0]
        out[:size] = first[...]
        out[size:] = second[...]


def join(core, own, got):
    rows, units = own[0].shape
    return small_kernel(put_together, core, [(2 * rows, units)] * 2, *own, *got)


def wide(value):
    return value.astype(jnp.float32)


def first_sum(core, mine_ref, got_ref, near_ref, far_ref, out_ref):
    for i in range(2):
        out_ref[i] = (wide(mine_ref[i]) + wide(got_ref[i])).astype(jnp.bfloat16)
    total = wide(mine_ref[core]) + wide(got_ref[core]) + wide(near_ref[0]) + wide(far_ref[0])
    out_ref[core] = total.astype(jnp.bfloat16)


def second_sum(core, mine_ref, got_ref, arrived_ref, out_ref):
    for i in range(2):
        total = wide(mine_ref[2 + i]) + wide(got_ref[2 + i]) + wide(arrived_ref[i])
        out_ref[i] = total.astype(jnp.bfloat16)


def third_sum(core, mine_ref, got_ref, arrived_ref, keep_ref, give_ref):
    for which, out_ref in ((core, keep_ref), (1 - core, give_ref)):
        total = wide(mine_ref[4 + which]) + wide(got_ref[4 + which]) + wide(arrived_ref[which])
        out_ref[...] = total.astype(jnp.bfloat16)


def last_sum(core, mine_ref, got_ref, near_ref, far_ref, out_ref):
    total = wide(mine_ref[6]) + wide(got_ref[6]) + wide(near_ref[...]) + wide(far_ref[...])
    out_ref[...] = total.astype(jnp.bfloat16)


def partial_kernel(parts, sub, slot_ref, w_ref, *refs):
    *out_refs, result, out_sem = refs[-6:]
    features = w_ref.shape[0]
    for i, (first, half) in enumerate(parts):
        for low_column, high_column in ((0, 2 * WIDE), (2 * WIDE, features)):
            columns = slice(low_column, high_column)
            result[i, :, columns] = lax.dot_general(
                refs[i][...],
                w_ref[columns, :],
                (((1,), (1,)), ((), ())),
                preferred_element_type=jnp.float32,
            ).astype(jnp.bfloat16)
            for p in range(PLACES):
                slot = slot_ref[half * ROWS + first + p]
                source = result.at[i, pl.ds(p * sub, sub), columns]
                for out_ref, low, high in zip(
                    out_refs, (0, 1, ZS, ZS + 1), (1, ZS, ZS + 1, 2 * ZS)
                ):

                    @pl.when((slot >= low) & (slot < high))
                    def _():
                        pltpu.make_async_copy(
                            source,
                            out_ref.at[slot - low, pl.ds(half * sub, sub), columns],
                            out_sem,
                        ).start()

    pltpu.make_async_copy(result, result, out_sem).wait()


def partial_sums(slots, parts, pieces, weight, into=()):
    sub = pieces[0].shape[0] // PLACES
    features = weight.shape[0]
    count = len(pieces)
    anywhere, vmem = pl.BlockSpec(memory_space=pl.ANY), pl.BlockSpec(memory_space=pltpu.VMEM)
    inputs = (weight, *pieces, *into)
    return pl.pallas_call(
        lambda *refs: partial_kernel(parts, sub, *refs),
        out_shape=[
            jax.ShapeDtypeStruct((n, 2 * sub, features), jnp.bfloat16)
            for n in (1, ZS - 1, 1, ZS - 1)
        ],
        in_specs=[pl.BlockSpec(memory_space=pltpu.SMEM)]
        + [vmem] * (1 + count)
        + [anywhere] * len(into),
        out_specs=[anywhere] * 4,
        scratch_shapes=[
            pltpu.VMEM((count, PLACES * sub, features), jnp.bfloat16),
            pltpu.SemaphoreType.DMA,
        ],
        input_output_aliases={2 + count + i: i for i in range(len(into))},
        compiler_params=pltpu.CompilerParams(vmem_limit_bytes=10 * MIB),
        cost_estimate=COST,
        name="partial_sums",
    )(slots, *inputs)


def turn_kernel(place_ref, *refs):
    sources, (out_ref, ordered) = refs[:-2], refs[-2:]
    total = ordered.shape[0]
    sub = total // (2 * ROWS)
    index = 0
    for source in sources:
        for b in range(source.shape[0]):
            for half in range(2):
                row = pl.multiple_of(place_ref[index] * sub, sub)
                ordered[pl.ds(row, sub), :] = source[b, half * sub : (half + 1) * sub, :]
                index += 1
    features = ordered.shape[1]
    for at in range(0, features, WIDE):
        size = min(WIDE, features - at)
        place = lambda axis: lax.broadcasted_iota(jnp.int32, (size, size), axis)
        one = jnp.where(place(0) == place(1), 1.0, 0.0).astype(jnp.bfloat16)
        out_ref[at : at + size, :] = lax.dot_general(
            one,
            ordered[:, at : at + size],
            (((1,), (1,)), ((), ())),
            preferred_element_type=jnp.float32,
        ).astype(jnp.bfloat16)


def turned_tokens(places, sources):
    features = sources[0].shape[-1]
    total = sum(source.shape[0] * source.shape[1] for source in sources)
    return pl.pallas_call(
        turn_kernel,
        out_shape=jax.ShapeDtypeStruct((features, total), jnp.bfloat16),
        grid_spec=pltpu.PrefetchScalarGridSpec(
            num_scalar_prefetch=1,
            grid=(),
            in_specs=[pl.BlockSpec(memory_space=pltpu.VMEM)] * len(sources),
            out_specs=pl.BlockSpec(memory_space=pltpu.VMEM),
            scratch_shapes=[pltpu.VMEM((total, features), jnp.bfloat16)],
        ),
        compiler_params=pltpu.CompilerParams(vmem_limit_bytes=14 * MIB),
        cost_estimate=pl.CostEstimate(flops=0, bytes_accessed=16_000_000, transcendentals=0),
        name="turned_tokens",
    )(places, *sources)


def weight_kernel(count, turned_ref, *refs):
    pieces, out_ref = refs[:count], refs[-1]
    sums, at = None, 0
    for piece in pieces:
        rows = piece.shape[0]
        term = jnp.dot(
            turned_ref[:, at : at + rows], piece[...], preferred_element_type=jnp.float32
        )
        sums = term if sums is None else sums + term
        at += rows
    out_ref[...] = sums.astype(jnp.bfloat16)


def weight_gradient(turned, pieces, begin, end, into=None):
    features, total = turned.shape
    units = pieces[0].shape[1]
    inputs = (turned, *pieces) + (() if into is None else (into,))
    return pl.pallas_call(
        lambda *refs: weight_kernel(len(pieces), *refs),
        out_shape=jax.ShapeDtypeStruct((features, units), jnp.bfloat16),
        grid=(end - begin,),
        in_specs=[pl.BlockSpec(memory_space=pltpu.VMEM)]
        + [pl.BlockSpec((piece.shape[0], WIDE), lambda n: (0, n + begin)) for piece in pieces]
        + [pl.BlockSpec(memory_space=pl.ANY)] * (into is not None),
        out_specs=pl.BlockSpec((features, WIDE), lambda n: (0, n + begin)),
        input_output_aliases={} if into is None else {1 + len(pieces): 0},
        compiler_params=pltpu.CompilerParams(vmem_limit_bytes=16 * MIB),
        cost_estimate=pl.CostEstimate(
            flops=2 * total * WIDE * (end - begin) * features,
            bytes_accessed=2_000_000 * (end - begin),
            transcendentals=0,
        ),
        name="weight_gradient",
    )(*inputs)


def shards(tokens, cotangent, preact, weight):
    row, col = lax.axis_index("row"), lax.axis_index("col")
    z, core = col // 2, col % 2
    size, features = tokens.shape
    sub = size // 2
    table = held()
    block = row ^ jnp.asarray(table)[core]
    to, parity = (block // 2 - z) % ZS, block % 2
    worker = jnp.where(to % 4 == 0, parity, to // 4)
    away = jnp.where(to > 4, ZS - to, to)
    slot = jnp.where(away == 4, 0, jnp.where(away == 0, 7, 7 - 2 * away + parity))
    slots = jnp.where(worker == core, slot, slot + ZS).reshape(-1).astype(jnp.int32)
    down = 2 * core - 1
    chips = [z] + [z + down * i for i in (1, 2, 3)]
    blocks = [(p % ZS) * 2 + c for p in chips for c in range(2)] + [(z + 4) % ZS * 2 + core]
    chips = [z - down * i for i in (1, 2, 3)]
    blocks += [(p % ZS) * 2 + c for p in chips for c in range(2)] + [(z + 4) % ZS * 2 + 1 - core]
    place = jnp.asarray(places_of(table))[core][:, jnp.stack(blocks) ^ row]
    start = (place // PLACES * 2 + jnp.arange(2)[:, None]) * PLACES + place % PLACES
    starts = start.T.reshape(-1).astype(jnp.int32)

    partner = swap(tokens, "token_pair")
    core = core.reshape(1).astype(jnp.int32)
    own = []
    for half in range(2):
        rows = slice(half * sub, (half + 1) * sub)
        values, slope_at = cotangent[rows], preact[rows]
        if half:
            values, slope_at, *own = lax.optimization_barrier((values, slope_at, *own))
        own.append((values.astype(jnp.float32) * gelu_slope(slope_at)).astype(jnp.bfloat16))
    got = [across(own[half], half, 0) for half in range(2)]
    (chip,) = small_kernel(pair_up, core, [(2, size, features)], tokens, partner)
    first = [across(own[half], half, 1) for half in range(2)]
    ring = [onward(chip, "tokens1")]
    *got, chip, slots, starts = lax.optimization_barrier((*got, chip, slots, starts))
    second = [across(got[half], half, 1) for half in range(2)]
    own = join(core, own, got)
    early = [across(own[half], half, 2) for half in range(2)]
    first, second, ring[0] = lax.optimization_barrier((first, second, ring[0]))
    got = join(core, first, second)
    own = join(core, own, got)
    late = [across(got[half], half, 2) for half in range(2)]
    ring.append(onward(ring[0], "tokens2"))
    both_halves = lambda first: ((first, 0), (first, 1))
    own, early = lax.optimization_barrier((own, early))
    near = [across(own[half], half, 3) for half in range(2)]
    sums = partial_sums(slots, both_halves(0), own, weight)
    early, late, ring[1], sums = lax.optimization_barrier((early, late, ring[1], sums))
    got = join(core, early, late)
    far = [across(got[half], half, 3) for half in range(2)]
    ring.append(onward(ring[1], "tokens3"))
    sums = partial_sums(slots, both_halves(4), got, weight, into=sums)
    near, sums = lax.optimization_barrier((near, sums))
    sums = partial_sums(slots, both_halves(8), near, weight, into=sums)
    far[0], ring, sums = lax.optimization_barrier((far[0], ring, sums))
    ring.append(
        onward(small_kernel(pick_one, core, [(1, size, features)], ring[2])[0], "tokens4")
    )
    for half in range(2):
        far[half], sums = lax.optimization_barrier((far[half], sums))
        sums = partial_sums(slots, ((12, half),), far[half : half + 1], weight, into=sums)
    mine_far, mine, other_far, other = sums
    pieces = [*own, *got, *near, *far]

    near = onward(mine_far, "sums1")
    far = permute(other_far, lambda r, z, c: (r, z - 1 + 2 * c, 1 - c), "sums1x")
    got = swap(other, "sum_swap")
    (passed,) = small_kernel(line_up, core, [(6, size, features)], *ring[:3])
    others = [swap(passed, "token_swap")]
    near, far, got = lax.optimization_barrier((near, far, got))
    pair = (2, size, features)
    (running,) = small_kernel(first_sum, core, [pair], mine, got, near, far)
    arrived = onward(running, "sums2")
    others.append(swap(ring[3], "last_swap"))
    token_arrays, _ = lax.optimization_barrier(([chip, *ring, *others], running))
    turned = turned_tokens(starts, token_arrays)
    arrived, turned = lax.optimization_barrier((arrived, turned))
    (running,) = small_kernel(second_sum, core, [pair], mine, got, arrived)
    arrived = onward(running, "sums3")
    turned, _ = lax.optimization_barrier((turned, running))
    tiles = pieces[0].shape[1] // WIDE
    part = tiles - tiles // 3
    weight_grad = weight_gradient(turned, pieces, 0, part)
    arrived, weight_grad, turned = lax.optimization_barrier((arrived, weight_grad, turned))
    keep, give = small_kernel(third_sum, core, [(size, features)] * 2, mine, got, arrived)
    near = onward(keep, "sums4")
    far = permute(give, lambda r, z, c: (r, z + 1 - 2 * c, 1 - c), "sums4x")
    turned, _ = lax.optimization_barrier((turned, keep))
    weight_grad = weight_gradient(turned, pieces, part, tiles, into=weight_grad)
    near, far, weight_grad = lax.optimization_barrier((near, far, weight_grad))
    (input_grad,) = small_kernel(last_sum, core, [(size, features)], mine, got, near, far)
    return input_grad, weight_grad


def solution(mesh):
    placed = (P("col", "row"), P("row", "col"), P("row", "col"), P("row", "col"))
    return jax.shard_map(
        shards,
        mesh=mesh,
        in_specs=placed,
        out_specs=(P("col", "row"), P("row", "col")),
        check_vma=False,
    )
```
